32 devices in a mesh: space: 8 (over z, y), chan: 4 (over x, core).
Axes of the slice: x: 2, y: 2, z: 4, core: 2. Of those that a mesh axis runs over, the one named last changes fastest.
Arguments:
- volume: bfloat16 [16, 32, 128, 128], P(None, 'space', 'chan'), may hold values from -6 to 6
- kernel: bfloat16 [27, 128, 128], P(None, None, 'chan'), may hold values from -0.109375 to 0.109375
- bias: float32 [128], P('chan'), may hold values from -3 to 3
- cotangent: bfloat16 [16, 32, 128, 128], P(None, 'space', 'chan'), may hold values from -6 to 6
Outputs:
- output: bfloat16 [16, 32, 128, 128], P(None, 'space', 'chan')
- volume_grad: bfloat16 [16, 32, 128, 128], P(None, 'space', 'chan')
The draws below stay inside these ranges and needn't reach their ends.
All inputs are finite; a program needn't handle non-finite values.
Results may differ from the reference program's by a relative error of at most 0.001.
Values may be sent and summed in bfloat16 or wider, within the bound.
A program may use at most 128 MiB of HBM per device.

```python
import jax
import jax.numpy as jnp

C = 128
X = 16
Z = 128
ROWS = 32


def levels(rng, dims, pieces, low, top_value):
    def one(axis_at, shards_of):
        heights = jax.random.uniform(jax.random.fold_in(jax.random.fold_in(rng, 6), axis_at), (shards_of,), jnp.float32, low / len(pieces), top_value / len(pieces))
        return jnp.repeat(jnp.exp(heights), dims[axis_at] // shards_of).reshape((-1,) + (1,) * (len(dims) - axis_at - 1))

    factor_of = one(*pieces[0])
    for cut in pieces[1:]:
        factor_of = factor_of * one(*cut)
    return factor_of


def noise(own_key, dims, spread, bound, shards=(), kind=jnp.bfloat16):
    drawn = spread * jax.random.normal(own_key, dims, jnp.float32)
    if shards:
        drawn = drawn * levels(own_key, dims, shards, -0.22, 0.18)
    return jnp.clip(drawn, -bound, bound).astype(kind)


def setup_inputs(seed: int = 0) -> dict:
    key_of = jax.random.split(jax.random.key(seed), 5)
    return {
        "volume": noise(key_of[0], (X, ROWS, C, Z), 1.0, 6.0, ((1, 8), (2, 4))),
        "kernel": noise(key_of[1], (27, C, C), (27 * C) ** -0.5, 0.109375, ((2, 4),)),
        "bias": noise(key_of[2], (C,), 0.5, 3.0, ((0, 4),), jnp.float32),
        "cotangent": noise(key_of[3], (X, ROWS, C, Z), 1.0, 6.0, ((1, 8), (2, 4))),
    }


def shifted_terms(padded, weights, forward, total):
    planes = padded.shape[0] - 2
    rows = padded.shape[1] - 2
    columns = padded.shape[3] - 2
    for offset in range(27):
        steps_at = (offset // 9, (offset // 3) % 3, offset % 3)
        if not forward:
            steps_at = (2 - steps_at[0], 2 - steps_at[1], 2 - steps_at[2])
        window = padded[steps_at[0]:steps_at[0] + planes, steps_at[1]:steps_at[1] + rows, :, steps_at[2]:steps_at[2] + columns]
        window = window.astype(jnp.float32)
        weight_now = weights[offset].astype(jnp.float32)
        if forward:
            total = total + jnp.einsum("xyiz,io->xyoz", window, weight_now)
        else:
            total = total + jnp.einsum("xyoz,io->xyiz", window, weight_now)
    return total


def reference(volume, kernel, bias, cotangent):
    padded = jnp.pad(volume, ((1, 1), (1, 1), (0, 0), (1, 1)))
    start = jnp.zeros(volume.shape, jnp.float32) + bias[None, None, :, None]
    output = shifted_terms(padded, kernel, True, start).astype(jnp.bfloat16)
    padded_grad = jnp.pad(cotangent, ((1, 1), (1, 1), (0, 0), (1, 1)))
    volume_grad = shifted_terms(padded_grad, kernel, False, jnp.zeros(volume.shape, jnp.float32))
    return output, volume_grad.astype(jnp.bfloat16)
```

```python
import functools

import jax
import jax.numpy as jnp
from jax import lax
from jax.experimental import pallas as pl
from jax.experimental.pallas import tpu as pltpu
from jax.sharding import PartitionSpec as P

MESH = pl.DeviceIdType.MESH


def convolve(padded, weights, start, out, first, last):
    rows = padded.shape[1] - 2
    channels, cells = padded.shape[2], padded.shape[3]
    block = weights.shape[0] // 3

    def plane(p, carry):
        total = None
        for a in range(3):
            right = jnp.concatenate(
                [
                    padded[p + a, r : r + 3].reshape(3 * channels, cells)
                    for r in range(rows)
                ],
                axis=1,
            )
            part = jnp.dot(
                weights[:, a * 3 * channels : (a + 1) * 3 * channels],
                right,
                preferred_element_type=jnp.float32,
            )
            total = part if total is None else total + part
        lane = lax.broadcasted_iota(jnp.int32, (block, cells), 1)
        for r in range(rows):
            piece = total[:, r * cells : (r + 1) * cells]
            low = pltpu.roll(piece[:block], 1, 1)
            high = pltpu.roll(piece[2 * block :], cells - 1, 1)
            result = piece[block : 2 * block]
            result = result + jnp.where(lane == 0, 0.0, low)
            result = result + jnp.where(lane == cells - 1, 0.0, high)
            if start is not None:
                result = result + start[...]
            out[p, r] = result.astype(out.dtype)
        return carry

    lax.fori_loop(first, last, plane, 0)


def body(
    n, count, volume, cotangent, near, far, bias,
    output, grad,
    v_pad, g_pad, far_all, far_turned,
    local_sem, w_send, w_recv, x_send, x_recv, s_send, s_recv, c_send, c_recv,
):
    s = lax.axis_index("space")
    c = lax.axis_index("chan")
    pairs = n // 2
    pair, side = c // 2, c % 2
    sibling = c + 1 - 2 * side
    planes, rows, block = volume.shape[0], volume.shape[1], volume.shape[2]
    has_low, has_high = s > 0, s < count - 1

    barrier = pltpu.get_barrier_semaphore()
    for j in range(1, n):
        pl.semaphore_signal(
            barrier, inc=1, device_id={"chan": lax.rem(c + j, n)}, device_id_type=MESH
        )

    @pl.when(has_low)
    def _():
        pl.semaphore_signal(barrier, inc=1, device_id={"space": s - 1}, device_id_type=MESH)

    @pl.when(has_high)
    def _():
        pl.semaphore_signal(barrier, inc=1, device_id={"space": s + 1}, device_id_type=MESH)

    peers = n - 1 + has_low.astype(jnp.int32) + has_high.astype(jnp.int32)
    pl.semaphore_wait(barrier, peers)

    def at(pad, first, size, owner):
        return pad.at[
            pl.ds(1, planes),
            pl.ds(first, size),
            pl.ds(pl.multiple_of(owner * block, block), block),
        ]

    spans = ((1, 1), (rows, 1), (2, rows - 2))
    sources = (volume, cotangent)
    pads = (v_pad, g_pad)

    def from_pair(j):
        return lax.rem(pair - j + pairs, pairs) * 2 + side

    def x_copy(t, j, i, arriving):
        first, size = spans[i]
        if arriving:
            src = dst = at(pads[t], first, size, from_pair(j))
        else:
            src = sources[t].at[:, pl.ds(first - 1, size)]
            dst = at(pads[t], first, size, c)
        return pltpu.make_async_remote_copy(
            src_ref=src, dst_ref=dst,
            send_sem=x_send.at[t, j - 1, i], recv_sem=x_recv.at[t, j - 1, i],
            device_id={"chan": lax.rem(pair + j, pairs) * 2 + side}, device_id_type=MESH,
        )

    def s_copy(t, j, way, arriving):
        landing = rows + 1 if way == 0 else 0
        owner = c if j == 0 else from_pair(j)
        dst = at(pads[t], landing, 1, owner)
        if arriving:
            src = dst
        elif j == 0:
            src = sources[t].at[:, pl.ds(0 if way == 0 else rows - 1, 1)]
        else:
            src = at(pads[t], 1 if way == 0 else rows, 1, owner)
        return pltpu.make_async_remote_copy(
            src_ref=src, dst_ref=dst,
            send_sem=s_send.at[t, j, way], recv_sem=s_recv.at[t, j, way],
            device_id={"space": s - 1 if way == 0 else s + 1}, device_id_type=MESH,
        )

    def c_copy(t, slot, arriving):
        reach = c if not arriving else sibling
        mine = reach % 2
        if slot == 0:
            dst = at(pads[t], 1, rows, reach)
            src = dst if arriving else sources[t]
        elif slot <= 3 * (pairs - 1):
            j, i = (slot - 1) // 3 + 1, (slot - 1) % 3
            owner = lax.rem(pair - j + pairs, pairs) * 2 + mine
            dst = src = at(pads[t], spans[i][0], spans[i][1], owner)
        else:
            rest = slot - 1 - 3 * (pairs - 1)
            j, way = rest // 2, rest % 2
            owner = lax.rem(pair - j + pairs, pairs) * 2 + mine
            dst = src = at(pads[t], rows + 1 if way == 0 else 0, 1, owner)
        return pltpu.make_async_remote_copy(
            src_ref=src, dst_ref=dst,
            send_sem=c_send.at[t, slot], recv_sem=c_recv.at[t, slot],
            device_id={"chan": sibling}, device_id_type=MESH,
        )

    def edge_slot(j, way):
        return 1 + 3 * (pairs - 1) + 2 * j + way

    def local(t):
        return pltpu.make_async_copy(sources[t], at(pads[t], 1, rows, c), local_sem.at[t])

    def w_copy(j, arriving):
        owner = lax.rem(c - j + n, n) if arriving else c
        target = lax.rem(c + j, n)
        dst = far_all.at[:, pl.ds(pl.multiple_of(owner * block, block), block)]
        return pltpu.make_async_remote_copy(
            src_ref=dst if arriving else far.at[target], dst_ref=dst,
            send_sem=w_send.at[j], recv_sem=w_recv.at[j],
            device_id={"chan": target}, device_id_type=MESH,
        )

    def sends_to(way):
        return has_low if way == 0 else has_high

    def gets_from(way):
        return has_high if way == 0 else has_low

    def when(flag, act):
        pl.when(flag)(act)

    def start_edges(t):
        for j in range(1, pairs):
            for i in (0, 1):
                x_copy(t, j, i, False).start()
        for way in (0, 1):
            when(sends_to(way), lambda way=way: s_copy(t, 0, way, False).start())

    def start_rest(t):
        for j in range(1, pairs):
            x_copy(t, j, 2, False).start()
        c_copy(t, 0, False).start()
        local(t).start()

    def pass_edges(t):
        for j in range(1, pairs):
            for way in (0, 1):
                x_copy(t, j, way, True).wait_recv()
                when(sends_to(way), lambda way=way, j=j: s_copy(t, j, way, False).start())
        for j in range(1, pairs):
            for way in (0, 1):
                c_copy(t, 1 + 3 * (j - 1) + way, False).start()

    def pass_halo(t, j):
        for way in (0, 1):

            def act(way=way):
                s_copy(t, j, way, True).wait_recv()
                c_copy(t, edge_slot(j, way), False).start()

            when(gets_from(way), act)

    def pass_middle(t):
        for j in range(1, pairs):
            x_copy(t, j, 2, True).wait_recv()
            c_copy(t, 3 * j, False).start()

    def collect(t):
        local(t).wait()
        for slot in range(1 + 3 * (pairs - 1)):
            c_copy(t, slot, True).wait_recv()
        for j in range(pairs):
            for way in (0, 1):
                when(
                    gets_from(way),
                    lambda way=way, j=j: c_copy(t, edge_slot(j, way), True).wait_recv(),
                )

    def finish(t):
        for j in range(1, pairs):
            for i in range(3):
                x_copy(t, j, i, False).wait_send()
        for slot in range(1 + 3 * (pairs - 1)):
            c_copy(t, slot, False).wait_send()
        for j in range(pairs):
            for way in (0, 1):
                when(sends_to(way), lambda way=way, j=j: s_copy(t, j, way, False).wait_send())
                when(
                    gets_from(way),
                    lambda way=way, j=j: c_copy(t, edge_slot(j, way), False).wait_send(),
                )

    start_edges(0)
    start_rest(0)
    own = pltpu.make_async_copy(
        far.at[c], far_all.at[:, pl.ds(pl.multiple_of(c * block, block), block)], local_sem.at[2]
    )
    own.start()
    for j in range(1, n):
        w_copy(j, False).start()

    for pad in pads:
        blank = jnp.zeros(pad.shape[1:], pad.dtype)
        pad[0] = blank
        pad[planes + 1] = blank

        @pl.when(jnp.logical_not(has_low))
        def _():
            pad[:, 0] = jnp.zeros((planes + 2,) + pad.shape[2:], pad.dtype)

        @pl.when(jnp.logical_not(has_high))
        def _():
            pad[:, rows + 1] = jnp.zeros((planes + 2,) + pad.shape[2:], pad.dtype)

    pass_edges(0)
    start_edges(1)
    pass_halo(0, 0)
    pass_middle(0)
    start_rest(1)
    for j in range(1, n):
        w_copy(j, True).wait_recv()
    own.wait()
    for k in range(9):
        depth = far_all.shape[1]
        far_turned[:, k * depth : (k + 1) * depth] = far_all[k].T[: 3 * block]
    for j in range(1, pairs):
        pass_halo(0, j)
    pass_edges(1)
    collect(0)
    half = planes // 2
    convolve(v_pad, near, bias, output, 0, half)
    pass_halo(1, 0)
    pass_middle(1)
    convolve(v_pad, near, bias, output, half, planes)
    for j in range(1, pairs):
        pass_halo(1, j)
    collect(1)
    convolve(g_pad, far_turned, None, grad, 0, planes)
    for j in range(1, n):
        w_copy(j, False).wait_send()
    finish(0)
    finish(1)


def per_device(n, count, volume, kernel, bias, cotangent):
    planes, rows, block, cells = volume.shape
    channels = kernel.shape[1]
    taps = kernel.reshape(3, 3, 3, channels, block)
    near = taps.transpose(2, 4, 0, 1, 3).reshape(3 * block, 9 * channels)
    far = taps[::-1, ::-1, ::-1].reshape(9, 3, n, block, block)
    far = far.transpose(2, 0, 4, 1, 3).reshape(n, 9, block, 3 * block)
    far = jnp.pad(far, ((0, 0), (0, 0), (0, 0), (0, channels - 3 * block)))
    wide_bias = jnp.broadcast_to(bias[:, None], (block, cells))
    pairs = n // 2
    slots = 1 + 3 * (pairs - 1) + 2 * pairs
    dma = pltpu.SemaphoreType.DMA
    padded = pltpu.VMEM((planes + 2, rows + 2, channels, cells), volume.dtype)
    whole = pl.BlockSpec(memory_space=pltpu.VMEM)
    shape = jax.ShapeDtypeStruct(volume.shape, volume.dtype)
    others = max(pairs - 1, 1)
    return pl.pallas_call(
        functools.partial(body, n, count),
        out_shape=(shape, shape),
        in_specs=[pl.BlockSpec(memory_space=pl.ANY)] * 2 + [whole] * 3,
        out_specs=(whole, whole),
        scratch_shapes=[
            padded,
            padded,
            pltpu.VMEM((9, channels, channels), kernel.dtype),
            pltpu.VMEM((3 * block, 9 * channels), kernel.dtype),
            dma((3,)),
            dma((n,)),
            dma((n,)),
            dma((2, others, 3)),
            dma((2, others, 3)),
            dma((2, pairs, 2)),
            dma((2, pairs, 2)),
            dma((2, slots)),
            dma((2, slots)),
        ],
        compiler_params=pltpu.CompilerParams(
            collective_id=0, has_side_effects=True, vmem_limit_bytes=48 * 1024 * 1024
        ),
        cost_estimate=pl.CostEstimate(
            flops=4 * 27 * planes * rows * cells * block * channels,
            bytes_accessed=4 * 2 * planes * rows * block * cells,
            transcendentals=0,
        ),
    )(volume, cotangent, near, far, wide_bias)


def solution(mesh):
    n, count = mesh.shape["chan"], mesh.shape["space"]
    spec = P(None, "space", "chan", None)
    return jax.shard_map(
        functools.partial(per_device, n, count),
        mesh=mesh,
        in_specs=(spec, P(None, None, "chan"), P("chan"), spec),
        out_specs=(spec, spec),
        check_vma=False,
    )
```

```python
import functools

import jax
import jax.numpy as jnp
from jax import lax
from jax.experimental import pallas as pl
from jax.experimental.pallas import tpu as pltpu
from jax.sharding import PartitionSpec as P

MESH = pl.DeviceIdType.MESH


def convolve(padded, weights, start, out, first, last):
    rows = padded.shape[1] - 2
    channels, cells = padded.shape[2], padded.shape[3]
    block = weights.shape[0] // 3

    def plane(p, carry):
        total = None
        for a in range(3):
            right = jnp.concatenate(
                [
                    padded[p + a, r : r + 3].reshape(3 * channels, cells)
                    for r in range(rows)
                ],
                axis=1,
            )
            part = jnp.dot(
                weights[:, a * 3 * channels : (a + 1) * 3 * channels],
                right,
                preferred_element_type=jnp.float32,
            )
            total = part if total is None else total + part
        lane = lax.broadcasted_iota(jnp.int32, (block, cells), 1)
        for r in range(rows):
            piece = total[:, r * cells : (r + 1) * cells]
            low = pltpu.roll(piece[:block], 1, 1)
            high = pltpu.roll(piece[2 * block :], cells - 1, 1)
            result = piece[block : 2 * block]
            result = result + jnp.where(lane == 0, 0.0, low)
            result = result + jnp.where(lane == cells - 1, 0.0, high)
            if start is not None:
                result = result + start[...]
            out[p, r] = result.astype(out.dtype)
        return carry

    lax.fori_loop(first, last, plane, 0)


def body(
    n, count, parts, volume, cotangent, turned_kernel, bias,
    output, grad,
    v_pad, g_pad, near, far, far_all, far_turned,
    local_sem, w_send, w_recv, x_send, x_recv, s_send, s_recv, c_send, c_recv,
):
    s = lax.axis_index("space")
    c = lax.axis_index("chan")
    pairs = n // 2
    pair, side = c // 2, c % 2
    sibling = c + 1 - 2 * side
    planes, rows, block = volume.shape[0], volume.shape[1], volume.shape[2]
    channels = turned_kernel.shape[2]
    has_low, has_high = s > 0, s < count - 1

    barrier = pltpu.get_barrier_semaphore()
    for j in range(1, n):
        pl.semaphore_signal(
            barrier, inc=1, device_id={"chan": lax.rem(c + j, n)}, device_id_type=MESH
        )

    @pl.when(has_low)
    def _():
        pl.semaphore_signal(barrier, inc=1, device_id={"space": s - 1}, device_id_type=MESH)

    @pl.when(has_high)
    def _():
        pl.semaphore_signal(barrier, inc=1, device_id={"space": s + 1}, device_id_type=MESH)

    peers = n - 1 + has_low.astype(jnp.int32) + has_high.astype(jnp.int32)
    pl.semaphore_wait(barrier, peers)

    sources = [(volume, cotangent)[part[0]] for part in parts]
    pads = [(v_pad, g_pad)[part[0]] for part in parts]

    def at(t, first, size, owner):
        return pads[t].at[
            pl.ds(1 + parts[t][1], parts[t][2]),
            pl.ds(first, size),
            pl.ds(pl.multiple_of(owner * block, block), block),
        ]

    def source(t, first, size):
        return sources[t].at[pl.ds(parts[t][1], parts[t][2]), pl.ds(first, size)]

    spans = ((1, 1), (rows, 1), (2, rows - 2))

    def from_pair(j):
        return lax.rem(pair - j + pairs, pairs) * 2 + side

    def x_copy(t, j, i, arriving):
        first, size = spans[i]
        if arriving:
            src = dst = at(t, first, size, from_pair(j))
        else:
            src = source(t, first - 1, size)
            dst = at(t, first, size, c)
        return pltpu.make_async_remote_copy(
            src_ref=src, dst_ref=dst,
            send_sem=x_send.at[t, j - 1, i], recv_sem=x_recv.at[t, j - 1, i],
            device_id={"chan": lax.rem(pair + j, pairs) * 2 + side}, device_id_type=MESH,
        )

    def s_copy(t, j, way, arriving):
        landing = rows + 1 if way == 0 else 0
        owner = c if j == 0 else from_pair(j)
        dst = at(t, landing, 1, owner)
        if arriving:
            src = dst
        elif j == 0:
            src = source(t, 0 if way == 0 else rows - 1, 1)
        else:
            src = at(t, 1 if way == 0 else rows, 1, owner)
        return pltpu.make_async_remote_copy(
            src_ref=src, dst_ref=dst,
            send_sem=s_send.at[t, j, way], recv_sem=s_recv.at[t, j, way],
            device_id={"space": s - 1 if way == 0 else s + 1}, device_id_type=MESH,
        )

    def c_copy(t, slot, arriving):
        reach = c if not arriving else sibling
        mine = reach % 2
        if slot == 0:
            dst = at(t, 1, rows, reach)
            src = dst if arriving else source(t, 0, rows)
        elif slot <= 3 * (pairs - 1):
            j, i = (slot - 1) // 3 + 1, (slot - 1) % 3
            owner = lax.rem(pair - j + pairs, pairs) * 2 + mine
            dst = src = at(t, spans[i][0], spans[i][1], owner)
        else:
            rest = slot - 1 - 3 * (pairs - 1)
            j, way = rest // 2, rest % 2
            owner = lax.rem(pair - j + pairs, pairs) * 2 + mine
            dst = src = at(t, rows + 1 if way == 0 else 0, 1, owner)
        return pltpu.make_async_remote_copy(
            src_ref=src, dst_ref=dst,
            send_sem=c_send.at[t, slot], recv_sem=c_recv.at[t, slot],
            device_id={"chan": sibling}, device_id_type=MESH,
        )

    def edge_slot(j, way):
        return 1 + 3 * (pairs - 1) + 2 * j + way

    def local(t):
        return pltpu.make_async_copy(source(t, 0, rows), at(t, 1, rows, c), local_sem.at[t])

    def w_copy(j, arriving):
        owner = lax.rem(c - j + n, n) if arriving else c
        target = lax.rem(c + j, n)
        dst = far_all.at[:, pl.ds(pl.multiple_of(owner * block, block), block)]
        return pltpu.make_async_remote_copy(
            src_ref=dst if arriving else far.at[target], dst_ref=dst,
            send_sem=w_send.at[j], recv_sem=w_recv.at[j],
            device_id={"chan": target}, device_id_type=MESH,
        )

    def sends_to(way):
        return has_low if way == 0 else has_high

    def gets_from(way):
        return has_high if way == 0 else has_low

    def when(flag, act):
        pl.when(flag)(act)

    def start_edges(t):
        for j in range(1, pairs):
            for i in (0, 1):
                x_copy(t, j, i, False).start()
        for way in (0, 1):
            when(sends_to(way), lambda way=way: s_copy(t, 0, way, False).start())

    def start_rest(t):
        for j in range(1, pairs):
            x_copy(t, j, 2, False).start()
        c_copy(t, 0, False).start()
        local(t).start()

    def pass_edges(t):
        for j in range(1, pairs):
            for way in (0, 1):
                x_copy(t, j, way, True).wait_recv()
                when(sends_to(way), lambda way=way, j=j: s_copy(t, j, way, False).start())
        for j in range(1, pairs):
            for way in (0, 1):
                c_copy(t, 1 + 3 * (j - 1) + way, False).start()

    def pass_halo(t, j):
        for way in (0, 1):

            def act(way=way):
                s_copy(t, j, way, True).wait_recv()
                c_copy(t, edge_slot(j, way), False).start()

            when(gets_from(way), act)

    def pass_middle(t):
        for j in range(1, pairs):
            x_copy(t, j, 2, True).wait_recv()
            c_copy(t, 3 * j, False).start()

    def collect(t):
        local(t).wait()
        for slot in range(1 + 3 * (pairs - 1)):
            c_copy(t, slot, True).wait_recv()
        for j in range(pairs):
            for way in (0, 1):
                when(
                    gets_from(way),
                    lambda way=way, j=j: c_copy(t, edge_slot(j, way), True).wait_recv(),
                )

    def finish(t):
        for j in range(1, pairs):
            for i in range(3):
                x_copy(t, j, i, False).wait_send()
        for slot in range(1 + 3 * (pairs - 1)):
            c_copy(t, slot, False).wait_send()
        for j in range(pairs):
            for way in (0, 1):
                when(sends_to(way), lambda way=way, j=j: s_copy(t, j, way, False).wait_send())
                when(
                    gets_from(way),
                    lambda way=way, j=j: c_copy(t, edge_slot(j, way), False).wait_send(),
                )

    for t in (0, 1):
        start_edges(t)
        start_rest(t)

    lane = lax.broadcasted_iota(jnp.int32, (block, channels), 1)
    for ab in range(9):
        packed = [jnp.zeros((block, channels), jnp.float32) for _ in range(n)]
        for q in range(3):
            turned = turned_kernel[26 - (3 * ab + q)].astype(jnp.float32)
            near_row, near_column = (2 - q) * block, (8 - ab) * channels
            near[near_row : near_row + block, near_column : near_column + channels] = (
                turned.astype(near.dtype)
            )
            inside = (lane >= q * block) & (lane < (q + 1) * block)
            for target in range(n):
                shift = (q - target) * block % channels
                moved = turned if shift == 0 else pltpu.roll(turned, shift, 1)
                packed[target] = jnp.where(inside, moved, packed[target])
        for target in range(n):
            far[target, ab] = packed[target].astype(far.dtype)
    own = pltpu.make_async_copy(
        far.at[c],
        far_all.at[:, pl.ds(pl.multiple_of(c * block, block), block)],
        local_sem.at[len(parts)],
    )
    own.start()
    for j in range(1, n):
        w_copy(j, False).start()

    for pad in (v_pad, g_pad):
        blank = jnp.zeros(pad.shape[1:], pad.dtype)
        pad[0] = blank
        pad[planes + 1] = blank

        @pl.when(jnp.logical_not(has_low))
        def _():
            pad[:, 0] = jnp.zeros((planes + 2,) + pad.shape[2:], pad.dtype)

        @pl.when(jnp.logical_not(has_high))
        def _():
            pad[:, rows + 1] = jnp.zeros((planes + 2,) + pad.shape[2:], pad.dtype)

    def pass_far(t):
        for j in range(1, pairs):
            pass_halo(t, j)

    split = parts[0][2] - 1
    middle = (split + planes) // 2
    g_split = parts[2][2] - 1
    pass_edges(0)
    pass_halo(0, 0)
    pass_middle(0)
    start_edges(2)
    start_rest(2)
    pass_edges(1)
    pass_halo(1, 0)
    pass_far(0)
    pass_middle(1)
    start_edges(3)
    start_rest(3)
    collect(0)
    convolve(v_pad, near, bias, output, 0, split)
    pass_edges(2)
    pass_halo(2, 0)
    pass_far(1)
    collect(1)
    convolve(v_pad, near, bias, output, split, middle)
    pass_middle(2)
    pass_edges(3)
    pass_halo(3, 0)
    convolve(v_pad, near, bias, output, middle, planes)
    pass_middle(3)
    pass_far(2)
    for j in range(1, n):
        w_copy(j, True).wait_recv()
    own.wait()
    for k in range(9):
        depth = far_all.shape[1]
        far_turned[:, k * depth : (k + 1) * depth] = far_all[k].T[: 3 * block]
    collect(2)
    pass_far(3)
    convolve(g_pad, far_turned, None, grad, 0, g_split)
    collect(3)
    convolve(g_pad, far_turned, None, grad, g_split, planes)
    for j in range(1, n):
        w_copy(j, False).wait_send()
    for t in range(len(parts)):
        finish(t)


def per_device(n, count, volume, kernel, bias, cotangent):
    planes, rows, block, cells = volume.shape
    channels = kernel.shape[1]
    wide_bias = jnp.broadcast_to(bias[:, None], (block, cells))
    half = planes // 2
    parts = [(t, first, size) for t in (0, 1) for first, size in ((0, half), (half, planes - half))]
    pairs = n // 2
    slots = 1 + 3 * (pairs - 1) + 2 * pairs
    dma = pltpu.SemaphoreType.DMA
    padded = pltpu.VMEM((planes + 2, rows + 2, channels, cells), volume.dtype)
    whole = pl.BlockSpec(memory_space=pltpu.VMEM)
    shape = jax.ShapeDtypeStruct(volume.shape, volume.dtype)
    others = max(pairs - 1, 1)
    return pl.pallas_call(
        functools.partial(body, n, count, parts),
        out_shape=(shape, shape),
        in_specs=[pl.BlockSpec(memory_space=pl.ANY)] * 2 + [whole] * 2,
        out_specs=(whole, whole),
        scratch_shapes=[
            padded,
            padded,
            pltpu.VMEM((3 * block, 9 * channels), kernel.dtype),
            pltpu.VMEM((n, 9, block, channels), kernel.dtype),
            pltpu.VMEM((9, channels, channels), kernel.dtype),
            pltpu.VMEM((3 * block, 9 * channels), kernel.dtype),
            dma((5,)),
            dma((n,)),
            dma((n,)),
            dma((4, others, 3)),
            dma((4, others, 3)),
            dma((4, pairs, 2)),
            dma((4, pairs, 2)),
            dma((4, slots)),
            dma((4, slots)),
        ],
        compiler_params=pltpu.CompilerParams(
            collective_id=0, has_side_effects=True, vmem_limit_bytes=48 * 1024 * 1024
        ),
        cost_estimate=pl.CostEstimate(
            flops=4 * 27 * planes * rows * cells * block * channels,
            bytes_accessed=4 * 2 * planes * rows * block * cells,
            transcendentals=0,
        ),
    )(volume, cotangent, kernel.transpose(0, 2, 1), wide_bias)


def solution(mesh):
    n, count = mesh.shape["chan"], mesh.shape["space"]
    spec = P(None, "space", "chan", None)
    return jax.shard_map(
        functools.partial(per_device, n, count),
        mesh=mesh,
        in_specs=(spec, P(None, None, "chan"), P("chan"), spec),
        out_specs=(spec, spec),
        check_vma=False,
    )
```

```python
import functools

import jax
import jax.numpy as jnp
from jax import lax
from jax.experimental import pallas as pl
from jax.experimental.pallas import tpu as pltpu
from jax.sharding import PartitionSpec as P

MESH = pl.DeviceIdType.MESH


def convolve(padded, weights, start, out, first, last):
    rows = padded.shape[1] - 2
    channels, cells = padded.shape[2], padded.shape[3]
    block = weights.shape[0] // 3

    def plane(p, carry):
        total = None
        for a in range(3):
            right = jnp.concatenate(
                [
                    padded[p + a, r : r + 3].reshape(3 * channels, cells)
                    for r in range(rows)
                ],
                axis=1,
            )
            part = jnp.dot(
                weights[:, a * 3 * channels : (a + 1) * 3 * channels],
                right,
                preferred_element_type=jnp.float32,
            )
            total = part if total is None else total + part
        lane = lax.broadcasted_iota(jnp.int32, (block, cells), 1)
        for r in range(rows):
            piece = total[:, r * cells : (r + 1) * cells]
            low = pltpu.roll(piece[:block], 1, 1)
            high = pltpu.roll(piece[2 * block :], cells - 1, 1)
            result = piece[block : 2 * block]
            result = result + jnp.where(lane == 0, 0.0, low)
            result = result + jnp.where(lane == cells - 1, 0.0, high)
            if start is not None:
                result = result + start[...]
            out[p, r] = result.astype(out.dtype)
        return carry

    lax.fori_loop(first, last, plane, 0)


def body(
    n, count, parts, volume, cotangent, kernel_in, bias,
    output, grad,
    turned_kernel, v_pad, g_pad, near, far, far_all, far_turned,
    local_sem, w_send, w_recv, x_send, x_recv, s_send, s_recv, c_send, c_recv,
):
    s = lax.axis_index("space")
    c = lax.axis_index("chan")
    pairs = n // 2
    pair, side = c // 2, c % 2
    sibling = c + 1 - 2 * side
    planes, rows, block = volume.shape[0], volume.shape[1], volume.shape[2]
    channels = turned_kernel.shape[2]
    fetch = pltpu.make_async_copy(kernel_in, turned_kernel, local_sem.at[len(parts) + 1])
    fetch.start()
    has_low, has_high = s > 0, s < count - 1

    sources = [(volume, cotangent)[part[0]] for part in parts]
    pads = [(v_pad, g_pad)[part[0]] for part in parts]

    def at(t, first, size, owner):
        return pads[t].at[
            pl.ds(1 + parts[t][1], parts[t][2]),
            pl.ds(first, size),
            pl.ds(pl.multiple_of(owner * block, block), block),
        ]

    def source(t, first, size):
        return sources[t].at[pl.ds(parts[t][1], parts[t][2]), pl.ds(first, size)]

    spans = ((1, 1), (rows, 1), (2, rows - 2))

    def from_pair(j):
        return lax.rem(pair - j + pairs, pairs) * 2 + side

    def x_copy(t, j, i, arriving):
        first, size = spans[i]
        if arriving:
            src = dst = at(t, first, size, from_pair(j))
        else:
            src = dst = at(t, first, size, c)
        return pltpu.make_async_remote_copy(
            src_ref=src, dst_ref=dst,
            send_sem=x_send.at[t, j - 1, i], recv_sem=x_recv.at[t, j - 1, i],
            device_id={"chan": lax.rem(pair + j, pairs) * 2 + side}, device_id_type=MESH,
        )

    def s_copy(t, j, way, arriving):
        landing = rows + 1 if way == 0 else 0
        owner = c if j == 0 else from_pair(j)
        dst = at(t, landing, 1, owner)
        if arriving:
            src = dst
        else:
            src = at(t, 1 if way == 0 else rows, 1, owner)
        return pltpu.make_async_remote_copy(
            src_ref=src, dst_ref=dst,
            send_sem=s_send.at[t, j, way], recv_sem=s_recv.at[t, j, way],
            device_id={"space": s - 1 if way == 0 else s + 1}, device_id_type=MESH,
        )

    def c_copy(t, slot, arriving):
        reach = c if not arriving else sibling
        mine = reach % 2
        if slot == 0:
            dst = src = at(t, 1, rows, reach)
        elif slot <= 3 * (pairs - 1):
            j, i = (slot - 1) // 3 + 1, (slot - 1) % 3
            owner = lax.rem(pair - j + pairs, pairs) * 2 + mine
            dst = src = at(t, spans[i][0], spans[i][1], owner)
        else:
            rest = slot - 1 - 3 * (pairs - 1)
            j, way = rest // 2, rest % 2
            owner = lax.rem(pair - j + pairs, pairs) * 2 + mine
            dst = src = at(t, rows + 1 if way == 0 else 0, 1, owner)
        return pltpu.make_async_remote_copy(
            src_ref=src, dst_ref=dst,
            send_sem=c_send.at[t, slot], recv_sem=c_recv.at[t, slot],
            device_id={"chan": sibling}, device_id_type=MESH,
        )

    def edge_slot(j, way):
        return 1 + 3 * (pairs - 1) + 2 * j + way

    def local(t):
        return pltpu.make_async_copy(source(t, 0, rows), at(t, 1, rows, c), local_sem.at[t])

    def w_copy(j, arriving):
        owner = lax.rem(c - j + n, n) if arriving else c
        target = lax.rem(c + j, n)
        dst = far_all.at[:, pl.ds(pl.multiple_of(owner * block, block), block)]
        return pltpu.make_async_remote_copy(
            src_ref=dst if arriving else far.at[target], dst_ref=dst,
            send_sem=w_send.at[j], recv_sem=w_recv.at[j],
            device_id={"chan": target}, device_id_type=MESH,
        )

    def sends_to(way):
        return has_low if way == 0 else has_high

    def gets_from(way):
        return has_high if way == 0 else has_low

    def when(flag, act):
        pl.when(flag)(act)

    def start_edges(t):
        for j in range(1, pairs):
            for i in (0, 1):
                x_copy(t, j, i, False).start()
        for way in (0, 1):
            when(sends_to(way), lambda way=way: s_copy(t, 0, way, False).start())

    def start_rest(t):
        for j in range(1, pairs):
            x_copy(t, j, 2, False).start()
        c_copy(t, 0, False).start()

    def pass_edges(t):
        for j in range(1, pairs):
            for way in (0, 1):
                x_copy(t, j, way, True).wait_recv()
                when(sends_to(way), lambda way=way, j=j: s_copy(t, j, way, False).start())
        for j in range(1, pairs):
            for way in (0, 1):
                c_copy(t, 1 + 3 * (j - 1) + way, False).start()

    def pass_halo(t, j):
        for way in (0, 1):

            def act(way=way):
                s_copy(t, j, way, True).wait_recv()
                c_copy(t, edge_slot(j, way), False).start()

            when(gets_from(way), act)

    def pass_middle(t):
        for j in range(1, pairs):
            x_copy(t, j, 2, True).wait_recv()
            c_copy(t, 3 * j, False).start()

    def collect(t):
        for slot in range(1 + 3 * (pairs - 1)):
            c_copy(t, slot, True).wait_recv()
        for j in range(pairs):
            for way in (0, 1):
                when(
                    gets_from(way),
                    lambda way=way, j=j: c_copy(t, edge_slot(j, way), True).wait_recv(),
                )

    def finish(t):
        for j in range(1, pairs):
            for i in range(3):
                x_copy(t, j, i, False).wait_send()
        for slot in range(1 + 3 * (pairs - 1)):
            c_copy(t, slot, False).wait_send()
        for j in range(pairs):
            for way in (0, 1):
                when(sends_to(way), lambda way=way, j=j: s_copy(t, j, way, False).wait_send())
                when(
                    gets_from(way),
                    lambda way=way, j=j: c_copy(t, edge_slot(j, way), False).wait_send(),
                )

    for t in range(4):
        local(t).start()

    barrier = pltpu.get_barrier_semaphore()
    for j in range(1, n):
        pl.semaphore_signal(
            barrier, inc=1, device_id={"chan": lax.rem(c + j, n)}, device_id_type=MESH
        )

    @pl.when(has_low)
    def _():
        pl.semaphore_signal(barrier, inc=1, device_id={"space": s - 1}, device_id_type=MESH)

    @pl.when(has_high)
    def _():
        pl.semaphore_signal(barrier, inc=1, device_id={"space": s + 1}, device_id_type=MESH)

    peers = n - 1 + has_low.astype(jnp.int32) + has_high.astype(jnp.int32)
    pl.semaphore_wait(barrier, peers)

    for t in range(4):
        local(t).wait()
        start_edges(t)
        start_rest(t)

    lane = lax.broadcasted_iota(jnp.int32, (block, channels), 1)
    fetch.wait()
    for ab in range(9):
        packed = [jnp.zeros((block, channels), jnp.float32) for _ in range(n)]
        for q in range(3):
            turned = turned_kernel[26 - (3 * ab + q)].astype(jnp.float32)
            near_row, near_column = (2 - q) * block, (8 - ab) * channels
            near[near_row : near_row + block, near_column : near_column + channels] = (
                turned.astype(near.dtype)
            )
            inside = (lane >= q * block) & (lane < (q + 1) * block)
            for target in range(n):
                shift = (q - target) * block % channels
                moved = turned if shift == 0 else pltpu.roll(turned, shift, 1)
                packed[target] = jnp.where(inside, moved, packed[target])
        for target in range(n):
            far[target, ab] = packed[target].astype(far.dtype)
    own = pltpu.make_async_copy(
        far.at[c],
        far_all.at[:, pl.ds(pl.multiple_of(c * block, block), block)],
        local_sem.at[len(parts)],
    )
    own.start()
    for j in range(1, n):
        w_copy(j, False).start()

    for pad in (v_pad, g_pad):
        blank = jnp.zeros(pad.shape[1:], pad.dtype)
        pad[0] = blank
        pad[planes + 1] = blank

        @pl.when(jnp.logical_not(has_low))
        def _():
            pad[:, 0] = jnp.zeros((planes + 2,) + pad.shape[2:], pad.dtype)

        @pl.when(jnp.logical_not(has_high))
        def _():
            pad[:, rows + 1] = jnp.zeros((planes + 2,) + pad.shape[2:], pad.dtype)

    def pass_far(t):
        for j in range(1, pairs):
            pass_halo(t, j)

    split = parts[0][2] - 1
    middle = (split + planes) // 2
    g_split = parts[2][2] - 1
    pass_edges(0)
    pass_halo(0, 0)
    pass_middle(0)
    pass_edges(1)
    pass_halo(1, 0)
    pass_far(0)
    pass_middle(1)
    collect(0)
    convolve(v_pad, near, bias, output, 0, split)
    pass_edges(2)
    pass_halo(2, 0)
    pass_far(1)
    collect(1)
    convolve(v_pad, near, bias, output, split, middle)
    pass_middle(2)
    pass_edges(3)
    pass_halo(3, 0)
    convolve(v_pad, near, bias, output, middle, planes)
    pass_middle(3)
    pass_far(2)
    for j in range(1, n):
        w_copy(j, True).wait_recv()
    own.wait()
    for k in range(9):
        depth = far_all.shape[1]
        far_turned[:, k * depth : (k + 1) * depth] = far_all[k].T[: 3 * block]
    collect(2)
    pass_far(3)
    convolve(g_pad, far_turned, None, grad, 0, g_split)
    collect(3)
    convolve(g_pad, far_turned, None, grad, g_split, planes)
    for j in range(1, n):
        w_copy(j, False).wait_send()
    for t in range(len(parts)):
        finish(t)


def per_device(n, count, volume, kernel, bias, cotangent):
    planes, rows, block, cells = volume.shape
    channels = kernel.shape[1]
    wide_bias = jnp.broadcast_to(bias[:, None], (block, cells))
    half = planes // 2
    parts = [(t, first, size) for t in (0, 1) for first, size in ((0, half), (half, planes - half))]
    pairs = n // 2
    slots = 1 + 3 * (pairs - 1) + 2 * pairs
    dma = pltpu.SemaphoreType.DMA
    padded = pltpu.VMEM((planes + 2, rows + 2, channels, cells), volume.dtype)
    whole = pl.BlockSpec(memory_space=pltpu.VMEM)
    shape = jax.ShapeDtypeStruct(volume.shape, volume.dtype)
    others = max(pairs - 1, 1)
    return pl.pallas_call(
        functools.partial(body, n, count, parts),
        out_shape=(shape, shape),
        in_specs=[pl.BlockSpec(memory_space=pl.ANY)] * 3 + [whole],
        out_specs=(whole, whole),
        scratch_shapes=[
            pltpu.VMEM((27, block, channels), kernel.dtype),
            padded,
            padded,
            pltpu.VMEM((3 * block, 9 * channels), kernel.dtype),
            pltpu.VMEM((n, 9, block, channels), kernel.dtype),
            pltpu.VMEM((9, channels, channels), kernel.dtype),
            pltpu.VMEM((3 * block, 9 * channels), kernel.dtype),
            dma((6,)),
            dma((n,)),
            dma((n,)),
            dma((4, others, 3)),
            dma((4, others, 3)),
            dma((4, pairs, 2)),
            dma((4, pairs, 2)),
            dma((4, slots)),
            dma((4, slots)),
        ],
        compiler_params=pltpu.CompilerParams(
            collective_id=0, has_side_effects=True, vmem_limit_bytes=62 * 1024 * 1024
        ),
        cost_estimate=pl.CostEstimate(
            flops=4 * 27 * planes * rows * cells * block * channels,
            bytes_accessed=4 * 2 * planes * rows * block * cells,
            transcendentals=0,
        ),
    )(volume, cotangent, kernel.transpose(0, 2, 1), wide_bias)


def solution(mesh):
    n, count = mesh.shape["chan"], mesh.shape["space"]
    spec = P(None, "space", "chan", None)
    return jax.shard_map(
        functools.partial(per_device, n, count),
        mesh=mesh,
        in_specs=(spec, P(None, None, "chan"), P("chan"), spec),
        out_specs=(spec, spec),
        check_vma=False,
    )
```

```python
import functools

import jax
import jax.numpy as jnp
from jax import lax
from jax.experimental import pallas as pl
from jax.experimental.pallas import tpu as pltpu
from jax.sharding import PartitionSpec as P

MESH = pl.DeviceIdType.MESH


def convolve(padded, weights, start, out, first, last):
    rows = padded.shape[1] - 2
    channels, cells = padded.shape[2], padded.shape[3]
    block = weights.shape[0] // 3

    def plane(p, carry):
        total = None
        for a in range(3):
            right = jnp.concatenate(
                [
                    padded[p + a, r : r + 3].reshape(3 * channels, cells)
                    for r in range(rows)
                ],
                axis=1,
            )
            part = jnp.dot(
                weights[:, a * 3 * channels : (a + 1) * 3 * channels],
                right,
                preferred_element_type=jnp.float32,
            )
            total = part if total is None else total + part
        lane = lax.broadcasted_iota(jnp.int32, (block, cells), 1)
        for r in range(rows):
            piece = total[:, r * cells : (r + 1) * cells]
            low = pltpu.roll(piece[:block], 1, 1)
            high = pltpu.roll(piece[2 * block :], cells - 1, 1)
            result = piece[block : 2 * block]
            result = result + jnp.where(lane == 0, 0.0, low)
            result = result + jnp.where(lane == cells - 1, 0.0, high)
            if start is not None:
                result = result + start[...]
            out[p, r] = result.astype(out.dtype)
        return carry

    lax.fori_loop(first, last, plane, 0)


def body(
    n, count, parts, volume, cotangent, kernel_in, bias_row,
    output, grad,
    turned_kernel, bias, v_pad, g_pad, near, far, far_all, far_turned,
    local_sem, w_send, w_recv, x_send, x_recv, s_send, s_recv, c_send, c_recv,
):
    s = lax.axis_index("space")
    c = lax.axis_index("chan")
    pairs = n // 2
    pair, side = c // 2, c % 2
    sibling = c + 1 - 2 * side
    planes, rows, block = volume.shape[0], volume.shape[1], volume.shape[2]
    channels = turned_kernel.shape[2]
    fetch = pltpu.make_async_copy(kernel_in, turned_kernel, local_sem.at[len(parts) + 1])
    fetch.start()
    has_low, has_high = s > 0, s < count - 1

    sources = [(volume, cotangent)[part[0]] for part in parts]
    pads = [(v_pad, g_pad)[part[0]] for part in parts]

    def at(t, first, size, owner):
        return pads[t].at[
            pl.ds(1 + parts[t][1], parts[t][2]),
            pl.ds(first, size),
            pl.ds(pl.multiple_of(owner * block, block), block),
        ]

    def source(t, first, size):
        return sources[t].at[pl.ds(parts[t][1], parts[t][2]), pl.ds(first, size)]

    spans = ((1, 1), (rows, 1), (2, rows - 2))

    def from_pair(j):
        return lax.rem(pair - j + pairs, pairs) * 2 + side

    def x_copy(t, j, i, arriving):
        first, size = spans[i]
        if arriving:
            src = dst = at(t, first, size, from_pair(j))
        else:
            src = dst = at(t, first, size, c)
        return pltpu.make_async_remote_copy(
            src_ref=src, dst_ref=dst,
            send_sem=x_send.at[t, j - 1, i], recv_sem=x_recv.at[t, j - 1, i],
            device_id={"chan": lax.rem(pair + j, pairs) * 2 + side}, device_id_type=MESH,
        )

    def s_copy(t, j, way, arriving):
        landing = rows + 1 if way == 0 else 0
        owner = c if j == 0 else from_pair(j)
        dst = at(t, landing, 1, owner)
        if arriving:
            src = dst
        else:
            src = at(t, 1 if way == 0 else rows, 1, owner)
        return pltpu.make_async_remote_copy(
            src_ref=src, dst_ref=dst,
            send_sem=s_send.at[t, j, way], recv_sem=s_recv.at[t, j, way],
            device_id={"space": s - 1 if way == 0 else s + 1}, device_id_type=MESH,
        )

    def c_copy(t, slot, arriving):
        reach = c if not arriving else sibling
        mine = reach % 2
        if slot == 0:
            dst = src = at(t, 1, rows, reach)
        elif slot <= 3 * (pairs - 1):
            j, i = (slot - 1) // 3 + 1, (slot - 1) % 3
            owner = lax.rem(pair - j + pairs, pairs) * 2 + mine
            dst = src = at(t, spans[i][0], spans[i][1], owner)
        else:
            rest = slot - 1 - 3 * (pairs - 1)
            j, way = rest // 2, rest % 2
            owner = lax.rem(pair - j + pairs, pairs) * 2 + mine
            dst = src = at(t, rows + 1 if way == 0 else 0, 1, owner)
        return pltpu.make_async_remote_copy(
            src_ref=src, dst_ref=dst,
            send_sem=c_send.at[t, slot], recv_sem=c_recv.at[t, slot],
            device_id={"chan": sibling}, device_id_type=MESH,
        )

    def edge_slot(j, way):
        return 1 + 3 * (pairs - 1) + 2 * j + way

    def local(t):
        return pltpu.make_async_copy(source(t, 0, rows), at(t, 1, rows, c), local_sem.at[t])

    def w_copy(j, arriving):
        owner = lax.rem(c - j + n, n) if arriving else c
        target = lax.rem(c + j, n)
        dst = far_all.at[:, pl.ds(pl.multiple_of(owner * block, block), block)]
        return pltpu.make_async_remote_copy(
            src_ref=dst if arriving else far.at[target], dst_ref=dst,
            send_sem=w_send.at[j], recv_sem=w_recv.at[j],
            device_id={"chan": target}, device_id_type=MESH,
        )

    def sends_to(way):
        return has_low if way == 0 else has_high

    def gets_from(way):
        return has_high if way == 0 else has_low

    def when(flag, act):
        pl.when(flag)(act)

    def start_edges(t):
        for j in range(1, pairs):
            for i in (0, 1):
                x_copy(t, j, i, False).start()
        for way in (0, 1):
            when(sends_to(way), lambda way=way: s_copy(t, 0, way, False).start())

    def start_rest(t):
        for j in range(1, pairs):
            x_copy(t, j, 2, False).start()
        c_copy(t, 0, False).start()

    def pass_edges(t):
        for j in range(1, pairs):
            for way in (0, 1):
                x_copy(t, j, way, True).wait_recv()
                when(sends_to(way), lambda way=way, j=j: s_copy(t, j, way, False).start())
        for j in range(1, pairs):
            for way in (0, 1):
                c_copy(t, 1 + 3 * (j - 1) + way, False).start()

    def pass_halo(t, j):
        for way in (0, 1):

            def act(way=way):
                s_copy(t, j, way, True).wait_recv()
                c_copy(t, edge_slot(j, way), False).start()

            when(gets_from(way), act)

    def pass_middle(t):
        for j in range(1, pairs):
            x_copy(t, j, 2, True).wait_recv()
            c_copy(t, 3 * j, False).start()

    def collect(t):
        for slot in range(1 + 3 * (pairs - 1)):
            c_copy(t, slot, True).wait_recv()
        for j in range(pairs):
            for way in (0, 1):
                when(
                    gets_from(way),
                    lambda way=way, j=j: c_copy(t, edge_slot(j, way), True).wait_recv(),
                )

    def finish(t):
        for j in range(1, pairs):
            for i in range(3):
                x_copy(t, j, i, False).wait_send()
        for slot in range(1 + 3 * (pairs - 1)):
            c_copy(t, slot, False).wait_send()
        for j in range(pairs):
            for way in (0, 1):
                when(sends_to(way), lambda way=way, j=j: s_copy(t, j, way, False).wait_send())
                when(
                    gets_from(way),
                    lambda way=way, j=j: c_copy(t, edge_slot(j, way), False).wait_send(),
                )

    for t in range(4):
        local(t).start()

    barrier = pltpu.get_barrier_semaphore()
    for j in range(1, n):
        pl.semaphore_signal(
            barrier, inc=1, device_id={"chan": lax.rem(c + j, n)}, device_id_type=MESH
        )

    @pl.when(has_low)
    def _():
        pl.semaphore_signal(barrier, inc=1, device_id={"space": s - 1}, device_id_type=MESH)

    @pl.when(has_high)
    def _():
        pl.semaphore_signal(barrier, inc=1, device_id={"space": s + 1}, device_id_type=MESH)

    peers = n - 1 + has_low.astype(jnp.int32) + has_high.astype(jnp.int32)
    pl.semaphore_wait(barrier, peers)

    for t in range(4):
        local(t).wait()
        start_edges(t)
        start_rest(t)

    square = (block, block)
    diagonal = lax.broadcasted_iota(jnp.int32, square, 0) == lax.broadcasted_iota(
        jnp.int32, square, 1
    )
    spread = jnp.where(diagonal, jnp.broadcast_to(bias_row[...], square), 0.0)
    bias[...] = jnp.broadcast_to(jnp.sum(spread, axis=1, keepdims=True), bias.shape)

    lane = lax.broadcasted_iota(jnp.int32, (block, channels), 1)
    fetch.wait()
    for ab in range(9):
        packed = [jnp.zeros((block, channels), jnp.float32) for _ in range(n)]
        for q in range(3):
            turned = turned_kernel[26 - (3 * ab + q)].astype(jnp.float32)
            near_row, near_column = (2 - q) * block, (8 - ab) * channels
            near[near_row : near_row + block, near_column : near_column + channels] = (
                turned.astype(near.dtype)
            )
            inside = (lane >= q * block) & (lane < (q + 1) * block)
            for target in range(n):
                shift = (q - target) * block % channels
                moved = turned if shift == 0 else pltpu.roll(turned, shift, 1)
                packed[target] = jnp.where(inside, moved, packed[target])
        for target in range(n):
            far[target, ab] = packed[target].astype(far.dtype)
    own = pltpu.make_async_copy(
        far.at[c],
        far_all.at[:, pl.ds(pl.multiple_of(c * block, block), block)],
        local_sem.at[len(parts)],
    )
    own.start()
    for j in range(1, n):
        w_copy(j, False).start()

    for pad in (v_pad, g_pad):
        blank = jnp.zeros(pad.shape[1:], pad.dtype)
        pad[0] = blank
        pad[planes + 1] = blank

        @pl.when(jnp.logical_not(has_low))
        def _():
            pad[:, 0] = jnp.zeros((planes + 2,) + pad.shape[2:], pad.dtype)

        @pl.when(jnp.logical_not(has_high))
        def _():
            pad[:, rows + 1] = jnp.zeros((planes + 2,) + pad.shape[2:], pad.dtype)

    def pass_far(t):
        for j in range(1, pairs):
            pass_halo(t, j)

    split = parts[0][2] - 1
    middle = (split + planes) // 2
    g_split = parts[2][2] - 1
    pass_edges(0)
    pass_halo(0, 0)
    pass_middle(0)
    pass_edges(1)
    pass_halo(1, 0)
    pass_far(0)
    pass_middle(1)
    collect(0)
    convolve(v_pad, near, bias, output, 0, split)
    pass_edges(2)
    pass_halo(2, 0)
    pass_far(1)
    collect(1)
    convolve(v_pad, near, bias, output, split, middle)
    pass_middle(2)
    pass_edges(3)
    pass_halo(3, 0)
    convolve(v_pad, near, bias, output, middle, planes)
    pass_middle(3)
    pass_far(2)
    for j in range(1, n):
        w_copy(j, True).wait_recv()
    own.wait()
    for k in range(9):
        depth = far_all.shape[1]
        far_turned[:, k * depth : (k + 1) * depth] = far_all[k].T[: 3 * block]
    collect(2)
    pass_far(3)
    convolve(g_pad, far_turned, None, grad, 0, g_split)
    collect(3)
    convolve(g_pad, far_turned, None, grad, g_split, planes)
    for j in range(1, n):
        w_copy(j, False).wait_send()
    for t in range(len(parts)):
        finish(t)


def per_device(n, count, volume, kernel, bias, cotangent):
    planes, rows, block, cells = volume.shape
    channels = kernel.shape[1]
    half = planes // 2
    parts = [(t, first, size) for t in (0, 1) for first, size in ((0, half), (half, planes - half))]
    pairs = n // 2
    slots = 1 + 3 * (pairs - 1) + 2 * pairs
    dma = pltpu.SemaphoreType.DMA
    padded = pltpu.VMEM((planes + 2, rows + 2, channels, cells), volume.dtype)
    whole = pl.BlockSpec(memory_space=pltpu.VMEM)
    shape = jax.ShapeDtypeStruct(volume.shape, volume.dtype)
    others = max(pairs - 1, 1)
    return pl.pallas_call(
        functools.partial(body, n, count, parts),
        out_shape=(shape, shape),
        in_specs=[pl.BlockSpec(memory_space=pl.ANY)] * 3 + [whole],
        out_specs=(whole, whole),
        scratch_shapes=[
            pltpu.VMEM((27, block, channels), kernel.dtype),
            pltpu.VMEM((block, cells), jnp.float32),
            padded,
            padded,
            pltpu.VMEM((3 * block, 9 * channels), kernel.dtype),
            pltpu.VMEM((n, 9, block, channels), kernel.dtype),
            pltpu.VMEM((9, channels, channels), kernel.dtype),
            pltpu.VMEM((3 * block, 9 * channels), kernel.dtype),
            dma((6,)),
            dma((n,)),
            dma((n,)),
            dma((4, others, 3)),
            dma((4, others, 3)),
            dma((4, pairs, 2)),
            dma((4, pairs, 2)),
            dma((4, slots)),
            dma((4, slots)),
        ],
        compiler_params=pltpu.CompilerParams(
            collective_id=0, has_side_effects=True, vmem_limit_bytes=62 * 1024 * 1024
        ),
        cost_estimate=pl.CostEstimate(
            flops=4 * 27 * planes * rows * cells * block * channels,
            bytes_accessed=4 * 2 * planes * rows * block * cells,
            transcendentals=0,
        ),
    )(volume, cotangent, kernel.transpose(0, 2, 1), bias.reshape(1, block))


def solution(mesh):
    n, count = mesh.shape["chan"], mesh.shape["space"]
    spec = P(None, "space", "chan", None)
    return jax.shard_map(
        functools.partial(per_device, n, count),
        mesh=mesh,
        in_specs=(spec, P(None, None, "chan"), P("chan"), spec),
        out_specs=(spec, spec),
        check_vma=False,
    )
```

```python
import functools

import jax
import jax.numpy as jnp
from jax import lax
from jax.experimental import pallas as pl
from jax.experimental.pallas import tpu as pltpu
from jax.sharding import PartitionSpec as P

MESH = pl.DeviceIdType.MESH


def convolve(padded, weights, start, out, first, last):
    rows = padded.shape[1] - 2
    channels, cells = padded.shape[2], padded.shape[3]
    block = weights.shape[0] // 3

    def plane(p, carry):
        total = None
        for a in range(3):
            right = jnp.concatenate(
                [
                    padded[p + a, r : r + 3].reshape(3 * channels, cells)
                    for r in range(rows)
                ],
                axis=1,
            )
            part = jnp.dot(
                weights[:, a * 3 * channels : (a + 1) * 3 * channels],
                right,
                preferred_element_type=jnp.float32,
            )
            total = part if total is None else total + part
        lane = lax.broadcasted_iota(jnp.int32, (block, cells), 1)
        for r in range(rows):
            piece = total[:, r * cells : (r + 1) * cells]
            low = pltpu.roll(piece[:block], 1, 1)
            high = pltpu.roll(piece[2 * block :], cells - 1, 1)
            result = piece[block : 2 * block]
            result = result + jnp.where(lane == 0, 0.0, low)
            result = result + jnp.where(lane == cells - 1, 0.0, high)
            if start is not None:
                result = result + start[...]
            out[p, r] = result.astype(out.dtype)
        return carry

    lax.fori_loop(first, last, plane, 0)


def body(
    n, count, parts, volume, cotangent, kernel_in, bias_row,
    output, grad,
    turned_kernel, bias, v_pad, g_pad, near, far, far_all, far_turned,
    local_sem, w_send, w_recv, x_send, x_recv, s_send, s_recv, c_send, c_recv,
):
    s = lax.axis_index("space")
    c = lax.axis_index("chan")
    pairs = n // 2
    pair, side = c // 2, c % 2
    sibling = c + 1 - 2 * side
    planes, rows, block = volume.shape[0], volume.shape[1], volume.shape[2]
    channels = turned_kernel.shape[2]
    fetch = pltpu.make_async_copy(kernel_in, turned_kernel, local_sem.at[len(parts) + 1])
    fetch.start()
    has_low, has_high = s > 0, s < count - 1

    sources = [(volume, cotangent)[part[0]] for part in parts]
    pads = [(v_pad, g_pad)[part[0]] for part in parts]

    def at(t, first, size, owner):
        return pads[t].at[
            pl.ds(1 + parts[t][1], parts[t][2]),
            pl.ds(first, size),
            pl.ds(pl.multiple_of(owner * block, block), block),
        ]

    def source(t, first, size):
        return sources[t].at[pl.ds(parts[t][1], parts[t][2]), pl.ds(first, size)]

    spans = ((1, 1), (rows, 1), (2, rows - 2))

    def from_pair(j):
        return lax.rem(pair - j + pairs, pairs) * 2 + side

    def x_copy(t, j, i, arriving):
        first, size = spans[i]
        if arriving:
            src = dst = at(t, first, size, from_pair(j))
        else:
            src = dst = at(t, first, size, c)
        return pltpu.make_async_remote_copy(
            src_ref=src, dst_ref=dst,
            send_sem=x_send.at[t, j - 1, i], recv_sem=x_recv.at[t, j - 1, i],
            device_id={"chan": lax.rem(pair + j, pairs) * 2 + side}, device_id_type=MESH,
        )

    def s_copy(t, j, way, arriving):
        landing = rows + 1 if way == 0 else 0
        owner = c if j == 0 else from_pair(j)
        dst = at(t, landing, 1, owner)
        if arriving:
            src = dst
        else:
            src = at(t, 1 if way == 0 else rows, 1, owner)
        return pltpu.make_async_remote_copy(
            src_ref=src, dst_ref=dst,
            send_sem=s_send.at[t, j, way], recv_sem=s_recv.at[t, j, way],
            device_id={"space": s - 1 if way == 0 else s + 1}, device_id_type=MESH,
        )

    def c_copy(t, slot, arriving):
        reach = c if not arriving else sibling
        mine = reach % 2
        if slot == 0:
            dst = src = at(t, 1, rows, reach)
        elif slot <= 3 * (pairs - 1):
            j, i = (slot - 1) // 3 + 1, (slot - 1) % 3
            owner = lax.rem(pair - j + pairs, pairs) * 2 + mine
            dst = src = at(t, spans[i][0], spans[i][1], owner)
        else:
            rest = slot - 1 - 3 * (pairs - 1)
            j, way = rest // 2, rest % 2
            owner = lax.rem(pair - j + pairs, pairs) * 2 + mine
            dst = src = at(t, rows + 1 if way == 0 else 0, 1, owner)
        return pltpu.make_async_remote_copy(
            src_ref=src, dst_ref=dst,
            send_sem=c_send.at[t, slot], recv_sem=c_recv.at[t, slot],
            device_id={"chan": sibling}, device_id_type=MESH,
        )

    def edge_slot(j, way):
        return 1 + 3 * (pairs - 1) + 2 * j + way

    def local(t):
        return pltpu.make_async_copy(source(t, 0, rows), at(t, 1, rows, c), local_sem.at[t])

    def w_copy(j, arriving):
        owner = lax.rem(c - j + n, n) if arriving else c
        target = lax.rem(c + j, n)
        dst = far_all.at[:, pl.ds(pl.multiple_of(owner * block, block), block)]
        return pltpu.make_async_remote_copy(
            src_ref=dst if arriving else far.at[target], dst_ref=dst,
            send_sem=w_send.at[j], recv_sem=w_recv.at[j],
            device_id={"chan": target}, device_id_type=MESH,
        )

    def sends_to(way):
        return has_low if way == 0 else has_high

    def gets_from(way):
        return has_high if way == 0 else has_low

    def when(flag, act):
        pl.when(flag)(act)

    def start_edges(t):
        for j in range(1, pairs):
            for i in (0, 1):
                x_copy(t, j, i, False).start()
        for way in (0, 1):
            when(sends_to(way), lambda way=way: s_copy(t, 0, way, False).start())

    def start_rest(t):
        for j in range(1, pairs):
            x_copy(t, j, 2, False).start()
        c_copy(t, 0, False).start()

    def pass_edges(t):
        for j in range(1, pairs):
            for way in (0, 1):
                x_copy(t, j, way, True).wait_recv()
                when(sends_to(way), lambda way=way, j=j: s_copy(t, j, way, False).start())
        for j in range(1, pairs):
            for way in (0, 1):
                c_copy(t, 1 + 3 * (j - 1) + way, False).start()

    def pass_halo(t, j):
        for way in (0, 1):

            def act(way=way):
                s_copy(t, j, way, True).wait_recv()
                c_copy(t, edge_slot(j, way), False).start()

            when(gets_from(way), act)

    def pass_middle(t):
        for j in range(1, pairs):
            x_copy(t, j, 2, True).wait_recv()
            c_copy(t, 3 * j, False).start()

    def collect(t):
        for slot in range(1 + 3 * (pairs - 1)):
            c_copy(t, slot, True).wait_recv()
        for j in range(pairs):
            for way in (0, 1):
                when(
                    gets_from(way),
                    lambda way=way, j=j: c_copy(t, edge_slot(j, way), True).wait_recv(),
                )

    def finish(t):
        for j in range(1, pairs):
            for i in range(3):
                x_copy(t, j, i, False).wait_send()
        for slot in range(1 + 3 * (pairs - 1)):
            c_copy(t, slot, False).wait_send()
        for j in range(pairs):
            for way in (0, 1):
                when(sends_to(way), lambda way=way, j=j: s_copy(t, j, way, False).wait_send())
                when(
                    gets_from(way),
                    lambda way=way, j=j: c_copy(t, edge_slot(j, way), False).wait_send(),
                )

    for t in range(4):
        local(t).start()

    barrier = pltpu.get_barrier_semaphore()
    for j in range(1, n):
        pl.semaphore_signal(
            barrier, inc=1, device_id={"chan": lax.rem(c + j, n)}, device_id_type=MESH
        )

    @pl.when(has_low)
    def _():
        pl.semaphore_signal(barrier, inc=1, device_id={"space": s - 1}, device_id_type=MESH)

    @pl.when(has_high)
    def _():
        pl.semaphore_signal(barrier, inc=1, device_id={"space": s + 1}, device_id_type=MESH)

    peers = n - 1 + has_low.astype(jnp.int32) + has_high.astype(jnp.int32)
    pl.semaphore_wait(barrier, peers)

    for t in range(4):
        local(t).wait()
        start_edges(t)
        start_rest(t)

    square = (block, block)
    diagonal = lax.broadcasted_iota(jnp.int32, square, 0) == lax.broadcasted_iota(
        jnp.int32, square, 1
    )
    spread = jnp.where(diagonal, jnp.broadcast_to(bias_row[...], square), 0.0)
    bias[...] = jnp.broadcast_to(jnp.sum(spread, axis=1, keepdims=True), bias.shape)

    lane = lax.broadcasted_iota(jnp.int32, (block, channels), 1)
    fetch.wait()
    for ab in range(9):
        packed = [jnp.zeros((block, channels), jnp.float32) for _ in range(n)]
        for q in range(3):
            turned = turned_kernel[26 - (3 * ab + q)].astype(jnp.float32)
            near_row, near_column = (2 - q) * block, (8 - ab) * channels
            near[near_row : near_row + block, near_column : near_column + channels] = (
                turned.astype(near.dtype)
            )
            inside = (lane >= q * block) & (lane < (q + 1) * block)
            for target in range(n):
                shift = (q - target) * block % channels
                moved = turned if shift == 0 else pltpu.roll(turned, shift, 1)
                packed[target] = jnp.where(inside, moved, packed[target])
        for target in range(n):
            far[target, ab] = packed[target].astype(far.dtype)
    own = pltpu.make_async_copy(
        far.at[c],
        far_all.at[:, pl.ds(pl.multiple_of(c * block, block), block)],
        local_sem.at[len(parts)],
    )
    own.start()
    for j in range(1, n):
        w_copy(j, False).start()

    for pad in (v_pad, g_pad):
        blank = jnp.zeros(pad.shape[1:], pad.dtype)
        pad[0] = blank
        pad[planes + 1] = blank

        @pl.when(jnp.logical_not(has_low))
        def _():
            pad[:, 0] = jnp.zeros((planes + 2,) + pad.shape[2:], pad.dtype)

        @pl.when(jnp.logical_not(has_high))
        def _():
            pad[:, rows + 1] = jnp.zeros((planes + 2,) + pad.shape[2:], pad.dtype)

    def pass_far(t):
        for j in range(1, pairs):
            pass_halo(t, j)

    split = parts[0][2] - 1
    middle = (split + planes) // 2
    g_split = parts[2][2] - 1
    pass_edges(0)
    pass_halo(0, 0)
    pass_middle(0)
    pass_edges(1)
    pass_halo(1, 0)
    pass_far(0)
    pass_middle(1)
    collect(0)
    convolve(v_pad, near, bias, output, 0, split)
    pass_edges(2)
    pass_halo(2, 0)
    pass_far(1)
    collect(1)
    convolve(v_pad, near, bias, output, split, middle)
    pass_middle(2)
    pass_edges(3)
    pass_halo(3, 0)
    convolve(v_pad, near, bias, output, middle, planes)
    pass_far(2)
    for j in range(1, n):
        w_copy(j, True).wait_recv()
    own.wait()
    for k in range(9):
        depth = far_all.shape[1]
        far_turned[:, k * depth : (k + 1) * depth] = far_all[k].T[: 3 * block]
    collect(2)
    g_middle = g_split // 2
    convolve(g_pad, far_turned, None, grad, 0, g_middle)
    pass_middle(3)
    pass_far(3)
    convolve(g_pad, far_turned, None, grad, g_middle, g_split)
    collect(3)
    convolve(g_pad, far_turned, None, grad, g_split, planes)
    for j in range(1, n):
        w_copy(j, False).wait_send()
    for t in range(len(parts)):
        finish(t)


def per_device(n, count, volume, kernel, bias, cotangent):
    planes, rows, block, cells = volume.shape
    channels = kernel.shape[1]
    half = planes // 2
    late = planes - planes * 3 // 8
    cuts = (half, late)
    parts = [(t, *span) for t in (0, 1) for span in ((0, cuts[t]), (cuts[t], planes - cuts[t]))]
    pairs = n // 2
    slots = 1 + 3 * (pairs - 1) + 2 * pairs
    dma = pltpu.SemaphoreType.DMA
    padded = pltpu.VMEM((planes + 2, rows + 2, channels, cells), volume.dtype)
    whole = pl.BlockSpec(memory_space=pltpu.VMEM)
    shape = jax.ShapeDtypeStruct(volume.shape, volume.dtype)
    others = max(pairs - 1, 1)
    return pl.pallas_call(
        functools.partial(body, n, count, parts),
        out_shape=(shape, shape),
        in_specs=[pl.BlockSpec(memory_space=pl.ANY)] * 3 + [whole],
        out_specs=(whole, whole),
        scratch_shapes=[
            pltpu.VMEM((27, block, channels), kernel.dtype),
            pltpu.VMEM((block, cells), jnp.float32),
            padded,
            padded,
            pltpu.VMEM((3 * block, 9 * channels), kernel.dtype),
            pltpu.VMEM((n, 9, block, channels), kernel.dtype),
            pltpu.VMEM((9, channels, channels), kernel.dtype),
            pltpu.VMEM((3 * block, 9 * channels), kernel.dtype),
            dma((6,)),
            dma((n,)),
            dma((n,)),
            dma((4, others, 3)),
            dma((4, others, 3)),
            dma((4, pairs, 2)),
            dma((4, pairs, 2)),
            dma((4, slots)),
            dma((4, slots)),
        ],
        compiler_params=pltpu.CompilerParams(
            collective_id=0, has_side_effects=True, vmem_limit_bytes=62 * 1024 * 1024
        ),
        cost_estimate=pl.CostEstimate(
            flops=4 * 27 * planes * rows * cells * block * channels,
            bytes_accessed=4 * 2 * planes * rows * block * cells,
            transcendentals=0,
        ),
    )(volume, cotangent, kernel.transpose(0, 2, 1), bias.reshape(1, block))


def solution(mesh):
    n, count = mesh.shape["chan"], mesh.shape["space"]
    spec = P(None, "space", "chan", None)
    return jax.shard_map(
        functools.partial(per_device, n, count),
        mesh=mesh,
        in_specs=(spec, P(None, None, "chan"), P("chan"), spec),
        out_specs=(spec, spec),
        check_vma=False,
    )
```
